32 devices in a mesh: row: 16 (over z, y, x), col: 2 (over core).
Axes of the slice: x: 2, y: 2, z: 4, core: 2. Of those that a mesh axis runs over, the one named last changes fastest.
Arguments:
- matrix: bfloat16 [6144, 6144], P('row', 'col'), may hold values from -6 to 6
- pattern: int32 [32, 32], P('row', 'col'), may hold values 0 or 1
- inverse: bfloat16 [2, 384, 384], P(None, None, 'col'), may hold values from -0.0625 to 0.0625
Outputs:
- factored: bfloat16 [6144, 6144], P('row', 'col')
The draws below stay inside these ranges and needn't reach their ends.
All inputs are finite; a program needn't handle non-finite values. No bound on the sum of `pattern` on one device may be relied on, other than what follows from the above.
Results may differ from the reference program's by a relative error of at most 0.0063.
Values may be sent and summed in bfloat16 or wider, within the bound.
A program may use at most 128 MiB of HBM per device.

```python
import jax
import jax.numpy as jnp
from jax import lax

BLK = 192
SN = 384
MSD = 1
NSD = 8
NSUP = 16
ORDER = 6144
N_ROW = 16
N_COL = 2


def set_ends(values, rng, low, largest):
    extent = values.shape
    index_at = [jax.random.randint(jax.random.fold_in(rng, axis), (), 0, extent[axis]) for axis in range(len(extent))]
    values = values.at[tuple(index_at)].set(low)
    longest = extent.index(max(extent))
    index_at[longest] = (index_at[longest] + 1) % extent[longest]
    return values.at[tuple(index_at)].set(largest)


def levels(rng, dims, pieces, smallest, top_value):
    factor_of, own = 1.0, jax.random.fold_in(rng, 6)
    for axis_at, parts in pieces:
        draws = jnp.exp(jax.random.uniform(jax.random.fold_in(own, axis_at), (parts,), jnp.float32, smallest / len(pieces), top_value / len(pieces)))
        factor_of = factor_of * jnp.repeat(draws, dims[axis_at] // parts).reshape([-1 if axis == axis_at else 1 for axis in range(len(dims))])
    return factor_of


def gaussian(rng, extent, spread, most, pieces=(), held_as=jnp.bfloat16):
    values = spread * jax.random.normal(rng, extent, jnp.float32)
    if pieces:
        values = values * levels(rng, extent, pieces, -0.22, 0.18)
    return jnp.clip(values, -most, most).astype(held_as)


def setup_inputs(seed: int = 0) -> dict:
    splits = jax.random.split(jax.random.key(seed), 4)
    matrix = gaussian(splits[0], (ORDER, ORDER), 1.0, 6.0, ((0, 16), (1, 2)))
    pattern = set_ends((jax.random.randint(splits[1], (2 * NSUP, 2 * NSUP), 0, 3) < 2).astype(jnp.int32), jax.random.fold_in(splits[1], 1), 0, 1)
    inverse = gaussian(splits[2], (2, SN, SN), (1.5 / SN), 0.0625, ((2, 2),))
    return {"matrix": matrix, "pattern": pattern, "inverse": inverse}


def apply_mask(values, mask):
    rows, cols = values.shape
    mask_rows, mask_cols = mask.shape
    shaped = values.reshape(mask_rows, rows // mask_rows, mask_cols, cols // mask_cols)
    return (shaped * mask[:, None, :, None].astype(values.dtype)).reshape(rows, cols)


def reference(matrix, pattern, inverse):
    nsup = MSD * N_ROW
    tile_width = 2 * BLK
    total = nsup * tile_width
    positions = jnp.arange(nsup, dtype=jnp.int32)
    row_tiles_label = (positions % MSD) * N_ROW + positions // MSD
    col_tiles_label = (positions % NSD) * N_COL + positions // NSD
    row_label = jnp.repeat(row_tiles_label, 2)
    col_label = jnp.repeat(col_tiles_label, 2)
    masked = apply_mask(matrix, pattern)

    def row_spot(panel_k):
        return (panel_k % N_ROW) * MSD + panel_k // N_ROW

    def col_spot(panel_k):
        return (panel_k % N_COL) * NSD + panel_k // N_COL

    def lower_factor(tile, panel_k):
        spot = col_spot(panel_k)
        keep_mask = pattern[:, 2 * spot:2 * spot + 2] * (row_label > panel_k).astype(jnp.int32)[:, None]
        product = jnp.dot(tile, inverse[panel_k], preferred_element_type=jnp.float32)
        return apply_mask(product, keep_mask).astype(jnp.bfloat16)

    def upper_keep(panel_k):
        return jnp.broadcast_to((col_label > panel_k).astype(jnp.int32)[None, :], (2, 2 * nsup))

    col_zero = col_spot(0)
    row_zero = row_spot(0)
    col_first = col_spot(1)
    row_first = row_spot(1)
    lower_first = lower_factor(masked[:, col_zero * tile_width:(col_zero + 1) * tile_width], 0)
    upper_first = apply_mask(masked[row_zero * tile_width:(row_zero + 1) * tile_width], upper_keep(0))
    column_one = masked[:, col_first * tile_width:(col_first + 1) * tile_width].astype(jnp.float32)
    column_one = column_one - jnp.dot(lower_first, upper_first[:, col_first * tile_width:(col_first + 1) * tile_width], preferred_element_type=jnp.float32)
    column_one = apply_mask(column_one, pattern[:, 2 * col_first:2 * col_first + 2]).astype(jnp.bfloat16)
    row_one = masked[row_first * tile_width:(row_first + 1) * tile_width].astype(jnp.float32)
    row_one = row_one - jnp.dot(lower_first[row_first * tile_width:(row_first + 1) * tile_width], upper_first, preferred_element_type=jnp.float32)
    row_one = apply_mask(row_one, pattern[2 * row_first:2 * row_first + 2]).astype(jnp.bfloat16)
    lower_second = lower_factor(column_one, 1)
    upper_second = apply_mask(row_one, upper_keep(1))
    lower_both = jnp.concatenate([lower_first, lower_second], axis=1)
    upper_both = jnp.concatenate([upper_first, upper_second], axis=0)
    tile_labels = col_tiles_label[None, None, :, None, None]

    def tile_view(values):
        return values.reshape(2, BLK, nsup, 2, BLK)

    def one_row(position):
        start = (position * tile_width).astype(jnp.int32)
        row_block = lax.dynamic_slice_in_dim(masked, start, tile_width, 0)
        left_part = lax.dynamic_slice_in_dim(lower_both, start, tile_width, 0)
        running = row_block.astype(jnp.float32) - jnp.dot(left_part, upper_both, preferred_element_type=jnp.float32)
        pattern_rows = lax.dynamic_slice_in_dim(pattern, (2 * position).astype(jnp.int32), 2, 0)
        rounded = apply_mask(running, pattern_rows).astype(jnp.bfloat16)
        label_here = row_tiles_label[position]
        low_one = lax.dynamic_slice_in_dim(lower_first, start, tile_width, 0).reshape(2, BLK, 1, 2, BLK)
        low_two = lax.dynamic_slice_in_dim(lower_second, start, tile_width, 0).reshape(2, BLK, 1, 2, BLK)
        result = tile_view(rounded)
        result = jnp.where((tile_labels == 1) & (label_here > 1), low_two, result)
        result = jnp.where((tile_labels >= 1) & (label_here == 1), tile_view(row_one), result)
        result = jnp.where((tile_labels == 0) & (label_here >= 1), low_one, result)
        result = jnp.where(label_here == 0, tile_view(row_block), result)
        return result.reshape(tile_width, total)

    return lax.map(one_row, positions).reshape(total, total)
```

```python
import functools

import jax
import jax.numpy as jnp
from jax import lax
from jax.experimental import pallas as pl
from jax.experimental.pallas import tpu as pltpu
from jax.sharding import PartitionSpec as P

TREES = 3
SPLIT = 2
LANES = 128
STRIP = 16
MESH = pl.DeviceIdType.MESH
BF16 = jnp.bfloat16
F32 = jnp.float32

PARENTS_16 = (
    (None, 0, 0, 2, 6, 7, 2, 6, 10, 11, 6, 10, 14, 15, 10, 14),
    (None, 3, 0, 2, 0, 4, 4, 3, 4, 8, 8, 10, 8, 12, 10, 14),
    (None, 0, 6, 7, 0, 4, 4, 6, 4, 8, 6, 9, 8, 12, 12, 13),
)


def grid_of(n_row):
    if n_row == 16:
        return (4, 2, 2)
    if n_row % 4 == 0 and n_row > 4:
        return (4, n_row // 4)
    return (n_row,)


def ordered_parents(n_row, root, order):
    dims = grid_of(n_row)
    strides = [1] * len(dims)
    for i in range(len(dims) - 2, -1, -1):
        strides[i] = strides[i + 1] * dims[i + 1]
    parents = [None] * n_row
    for r in range(n_row):
        for i in order:
            here, there = (r // strides[i]) % dims[i], (root // strides[i]) % dims[i]
            if here != there:
                parents[r] = r + (strides[i] if there > here else -strides[i])
                break
    return parents


def all_trees(n_row):
    if n_row == 16:
        first = [list(p) for p in PARENTS_16]
        second = [[None if p[r ^ 1] is None else p[r ^ 1] ^ 1 for r in range(16)] for p in first]
        return first + second
    axes = list(range(len(grid_of(n_row))))
    orders = [axes if t % 2 == 0 else axes[::-1] for t in range(TREES)]
    return [ordered_parents(n_row, root, order) for root in (0, 1) for order in orders]


def pack_tree(parents):
    n_row = len(parents)
    packed, depths = [], []
    for r in range(n_row):
        depth, at = 0, r
        while parents[at] is not None:
            depth, at = depth + 1, parents[at]
        children = [c for c in range(n_row) if parents[c] == r]
        assert len(children) <= 3 and n_row <= 64 and depth < 32
        padded = children + [r] * (3 - len(children))
        packed.append(depth + 32 * (len(children) + 4 * (padded[0] + 64 * (padded[1] + 64 * padded[2]))))
        depths.append(depth)
    return packed, max(depths)


def select(values, index):
    out = jnp.int32(values[0])
    for i in range(1, len(values)):
        out = jnp.where(index == i, jnp.int32(values[i]), out)
    return out


def kernel(
    n_row, n_col, width, m_ref, pat_ref, inv_ref, out_ref,
    ua, ub, mask, l1, l11, l2, invb,
    recv_sem, send_sem, x_recv, x_send, inv_recv, inv_send, own_sem,
):
    row, col = lax.axis_index("row"), lax.axis_index("col")
    rows, cols = m_ref.shape
    half = rows // 2
    slabs = cols // LANES
    per_tile = width // LANES
    tiles = cols // width
    steps = slabs // TREES * SPLIT

    barrier = pltpu.get_barrier_semaphore()
    dims = grid_of(n_row)
    expected = jnp.int32(n_col - 1)
    stride = n_row
    for size in dims:
        stride = stride // size
        place = (row // stride) % size
        for ok, other in ((place > 0, row - stride), (place < size - 1, row + stride)):
            expected = expected + ok.astype(jnp.int32)

            @pl.when(ok)
            def _(other=other):
                pl.semaphore_signal(barrier, inc=1, device_id={"row": other}, device_id_type=MESH)

    for c in range(n_col):
        @pl.when(col != c)
        def _(c=c):
            pl.semaphore_signal(barrier, inc=1, device_id={"col": jnp.int32(c)}, device_id_type=MESH)

    wide = (pat_ref.shape[1], cols)
    block = cols // pat_ref.shape[1]
    lane = lax.broadcasted_iota(jnp.int32, wide, 1)
    first = lax.broadcasted_iota(jnp.int32, wide, 0) * block
    spread = jnp.where((lane >= first) & (lane < first + block), 1.0, 0.0).astype(BF16)
    mask[...] = jnp.dot(pat_ref[...].astype(F32).astype(BF16), spread, preferred_element_type=F32)

    def source(dst, strip):
        for s in range(slabs):
            at = slice(s * LANES, (s + 1) * LANES)
            for h in range(2):
                keep = mask[h:h + 1, at]
                dst[s, h, 0:half, :] = (m_ref[h * half:(h + 1) * half, at].astype(F32) * keep).astype(BF16)
                if strip:
                    dst[s, h, half:half + STRIP, :] = jnp.broadcast_to(keep, (STRIP, LANES)).astype(BF16)

    @pl.when(row == 0)
    def _():
        source(ua, False)

    @pl.when(row == 1)
    def _():
        source(ub, True)

    pl.semaphore_wait(barrier, expected)

    shard = inv_ref.shape[1]
    for k in range(2):
        mine = invb.at[pl.ds(pl.multiple_of(col * shard, 16), shard)]

        @pl.when(col != k)
        def _(k=k, mine=mine):
            pltpu.make_async_remote_copy(
                inv_ref.at[k], mine, inv_send.at[k], inv_recv.at[col],
                device_id={"col": jnp.int32(k)}, device_id_type=MESH,
            ).start()

        @pl.when(col == k)
        def _(k=k, mine=mine):
            pltpu.make_async_copy(inv_ref.at[k], mine, own_sem).start()

    def wait_inverse():
        pltpu.make_async_copy(
            inv_ref.at[0], invb.at[pl.ds(pl.multiple_of(col * shard, 16), shard)], own_sem
        ).wait()
        for c in range(n_col):
            @pl.when(col != c)
            def _(c=c):
                pltpu.make_async_remote_copy(
                    inv_ref.at[0], invb.at[pl.ds(c * shard, shard)], inv_send.at[0], inv_recv.at[c],
                    device_id={"col": jnp.int32(c)}, device_id_type=MESH,
                ).wait_recv()

    def to_columns(buffer, which, root, act):
        for c in range(n_col):
            if c != root:
                act(pltpu.make_async_remote_copy(
                    buffer, buffer, x_send.at[which, c], x_recv.at[which],
                    device_id={"col": jnp.int32(c)}, device_id_type=MESH,
                ))

    def from_column(buffer, which, root):
        @pl.when(col != root)
        def _():
            pltpu.make_async_remote_copy(
                buffer, buffer, x_send.at[which, root], x_recv.at[which],
                device_id={"col": jnp.int32(root)}, device_id_type=MESH,
            ).wait_recv()

    def tile_of(ref, j):
        halves = [
            jnp.concatenate([ref[per_tile * j + i, h, 0:half, :] for i in range(per_tile)], axis=1)
            for h in range(2)
        ]
        return jnp.concatenate(halves, axis=0)

    def two(top, bottom):
        return jnp.concatenate(
            [jnp.broadcast_to(top, (half, width)), jnp.broadcast_to(bottom, (half, width))], axis=0
        )

    def columns(j):
        return pl.ds(pl.multiple_of(j * width, width), width)

    def mask_of(j):
        keep = mask[:, columns(j)]
        return two(keep[0:1], keep[1:2])

    def upper_mask(j):
        strips = [
            jnp.concatenate(
                [ub[per_tile * j + i, h, half:half + STRIP, :].astype(F32)[0:1] for i in range(per_tile)], axis=1
            )
            for h in range(2)
        ]
        return two(*strips)

    def dot(a, b):
        return jnp.dot(a, b, preferred_element_type=F32)

    def dot_t(a, b):
        return lax.dot_general(a, b, (((1,), (1,)), ((), ())), preferred_element_type=F32)

    def make_l1():
        @pl.when(col < 2)
        def _():
            wait_inverse()

        @pl.when(col == 0)
        def _():
            keep = mask_of(0)
            tile = (m_ref[:, 0:width].astype(F32) * keep).astype(BF16)
            alive = (row > 0).astype(F32)
            l1[...] = (dot_t(tile, invb[...]) * (keep * alive)).astype(BF16)
            to_columns(l1, 0, 0, lambda copy: copy.start())

    def make_l2():
        @pl.when(col == 0)
        def _():
            l11[...] = (dot_t(tile_of(ub, 0), invb[...]) * upper_mask(0)).astype(BF16)
            to_columns(l11, 1, 0, lambda copy: copy.start())

        from_column(l1, 0, 0)

        @pl.when(col == 1)
        def _():
            keep = mask_of(0)
            one = ((m_ref[:, 0:width].astype(F32) - dot(l1[...], tile_of(ua, 0))) * keep).astype(BF16)
            alive = (row > 1).astype(F32)
            l2[...] = (dot_t(one, invb[...]) * (keep * alive)).astype(BF16)
            to_columns(l2, 2, 1, lambda copy: copy.start())

    def update(j):
        upper = tile_of(ua, j)
        row_one = ((tile_of(ub, j).astype(F32) - dot(l11[...], upper)) * upper_mask(j)).astype(BF16)
        total = m_ref[:, columns(j)].astype(F32) - dot(l1[...], upper) - dot(l2[...], row_one)
        out_ref[:, columns(j)] = (total * mask_of(j)).astype(BF16)

    plans, deepest = [], 0
    for t, parents in enumerate(all_trees(n_row)):
        packed, depth = pack_tree(parents)
        deepest = max(deepest, depth)
        code = select(packed, row)
        depth, code = code % 32, code // 32
        count, code = code % 4, code // 4
        plans.append((t, depth, count, (code % 64, (code // 64) % 64, code // 4096)))

    def chunk(t, k):
        buffer = ua if t < TREES else ub
        slab = TREES * (k // SPLIT) + t % TREES
        return buffer.at[slab] if SPLIT == 1 else buffer.at[slab, k % SPLIT]

    def tree_copy(t, k, j, target):
        return pltpu.make_async_remote_copy(
            chunk(t, k), chunk(t, k), send_sem.at[t, j], recv_sem.at[t, k],
            device_id={"row": target}, device_id_type=MESH,
        )

    @pl.loop(0, steps + deepest + 1)
    def _(now):
        for i in range(2 * TREES):
            t, depth, count, children = plans[(i % 2) * TREES + i // 2]
            k = now - depth

            @pl.when((k >= 0) & (k < steps))
            def _(t=t, depth=depth, count=count, children=children, k=k):
                @pl.when(depth > 0)
                def _():
                    tree_copy(t, k, 0, children[0]).wait_recv()

                for j in range(3):
                    @pl.when(count > j)
                    def _(j=j):
                        tree_copy(t, k, j, children[j]).start()

        @pl.when(now == 1)
        def _():
            make_l1()

        done = now - (SPLIT + deepest)

        @pl.when(done == -1)
        def _():
            make_l2()

        @pl.when(done == 0)
        def _():
            from_column(l11, 1, 0)
            from_column(l2, 2, 1)

        @pl.when((done >= 0) & (done % SPLIT == 0))
        def _():
            update(done // SPLIT)

    @pl.when((col == 0) & (row >= 1))
    def _():
        out_ref[:, 0:width] = l1[...]

    @pl.when((col == 1) & (row >= 2))
    def _():
        out_ref[:, 0:width] = l2[...]

    for t, depth, count, children in plans:
        buffer = ua if t < TREES else ub
        whole = buffer.at[0:slabs // TREES]
        for j in range(3):
            @pl.when(count > j)
            def _(t=t, j=j, whole=whole, children=children):
                pltpu.make_async_remote_copy(
                    whole, whole, send_sem.at[t, j], recv_sem.at[t, 0],
                    device_id={"row": children[j]}, device_id_type=MESH,
                ).wait_send()

    for k in range(2):
        @pl.when(col != k)
        def _(k=k):
            pltpu.make_async_remote_copy(
                inv_ref.at[k], invb.at[0:shard], inv_send.at[k], inv_recv.at[0],
                device_id={"col": jnp.int32(k)}, device_id_type=MESH,
            ).wait_send()

    @pl.when(col == 0)
    def _():
        to_columns(l1, 0, 0, lambda copy: copy.wait_send())
        to_columns(l11, 1, 0, lambda copy: copy.wait_send())

    @pl.when(col == 1)
    def _():
        to_columns(l2, 2, 1, lambda copy: copy.wait_send())


def solution(mesh):
    n_row, n_col = mesh.shape["row"], mesh.shape["col"]

    def shards(matrix, pattern, inverse):
        rows, cols = matrix.shape
        width = inverse.shape[1]
        half = rows // 2
        slabs = cols // LANES
        steps = slabs // TREES * SPLIT
        turned = jnp.swapaxes(inverse, 1, 2)
        flops = 2 * rows * cols * width * 3
        return pl.pallas_call(
            functools.partial(kernel, n_row, n_col, width),
            out_shape=jax.ShapeDtypeStruct(matrix.shape, BF16),
            in_specs=[pl.BlockSpec(memory_space=pltpu.VMEM)] * 3,
            out_specs=pl.BlockSpec(memory_space=pltpu.VMEM),
            scratch_shapes=[
                pltpu.VMEM((slabs, 2, half, LANES), BF16),
                pltpu.VMEM((slabs, 2, half + STRIP, LANES), BF16),
                pltpu.VMEM((2, cols), F32),
                pltpu.VMEM((rows, width), BF16),
                pltpu.VMEM((width, width), BF16),
                pltpu.VMEM((rows, width), BF16),
                pltpu.VMEM((width, width), BF16),
                pltpu.SemaphoreType.DMA((2 * TREES, steps)),
                pltpu.SemaphoreType.DMA((2 * TREES, 3)),
                pltpu.SemaphoreType.DMA((3,)),
                pltpu.SemaphoreType.DMA((3, n_col)),
                pltpu.SemaphoreType.DMA((n_col,)),
                pltpu.SemaphoreType.DMA((2,)),
                pltpu.SemaphoreType.DMA,
            ],
            compiler_params=pltpu.CompilerParams(
                collective_id=0, has_side_effects=True, vmem_limit_bytes=48 * 1024 * 1024
            ),
            cost_estimate=pl.CostEstimate(flops=flops, bytes_accessed=4 * rows * cols, transcendentals=0),
        )(matrix, pattern, turned)

    return jax.shard_map(
        shards,
        mesh=mesh,
        in_specs=(P("row", "col"), P("row", "col"), P(None, None, "col")),
        out_specs=P("row", "col"),
        check_vma=False,
    )
```

```python
import functools

import jax
import jax.numpy as jnp
from jax import lax
from jax.experimental import pallas as pl
from jax.experimental.pallas import tpu as pltpu
from jax.sharding import PartitionSpec as P

TREES = 3
SPLIT = 4
LAG = 4
LANES = 128
STRIP = 16
MESH = pl.DeviceIdType.MESH
BF16 = jnp.bfloat16
F32 = jnp.float32

PARENTS_16 = (
    (None, 0, 0, 2, 6, 7, 2, 6, 10, 11, 6, 10, 14, 15, 10, 14),
    (None, 3, 0, 2, 0, 4, 4, 3, 4, 8, 8, 10, 8, 12, 10, 14),
    (None, 0, 6, 7, 0, 4, 4, 6, 4, 8, 6, 9, 8, 12, 12, 13),
)


def grid_of(n_row):
    if n_row == 16:
        return (4, 2, 2)
    if n_row % 4 == 0 and n_row > 4:
        return (4, n_row // 4)
    return (n_row,)


def ordered_parents(n_row, root, order):
    dims = grid_of(n_row)
    strides = [1] * len(dims)
    for i in range(len(dims) - 2, -1, -1):
        strides[i] = strides[i + 1] * dims[i + 1]
    parents = [None] * n_row
    for r in range(n_row):
        for i in order:
            here, there = (r // strides[i]) % dims[i], (root // strides[i]) % dims[i]
            if here != there:
                parents[r] = r + (strides[i] if there > here else -strides[i])
                break
    return parents


def all_trees(n_row):
    if n_row == 16:
        first = [list(p) for p in PARENTS_16]
        second = [[None if p[r ^ 1] is None else p[r ^ 1] ^ 1 for r in range(16)] for p in first]
        return first + second
    axes = list(range(len(grid_of(n_row))))
    orders = [axes if t % 2 == 0 else axes[::-1] for t in range(TREES)]
    return [ordered_parents(n_row, root, order) for root in (0, 1) for order in orders]


def pack_tree(parents):
    n_row = len(parents)
    packed, depths = [], []
    for r in range(n_row):
        depth, at = 0, r
        while parents[at] is not None:
            depth, at = depth + 1, parents[at]
        children = [c for c in range(n_row) if parents[c] == r]
        assert len(children) <= 3 and n_row <= 64 and depth < 32
        padded = children + [r] * (3 - len(children))
        packed.append(depth + 32 * (len(children) + 4 * (padded[0] + 64 * (padded[1] + 64 * padded[2]))))
        depths.append(depth)
    return packed, max(depths)


def select(values, index):
    out = jnp.int32(values[0])
    for i in range(1, len(values)):
        out = jnp.where(index == i, jnp.int32(values[i]), out)
    return out


def kernel(
    n_row, n_col, width, m_hbm, pat_hbm, inv_ref, out_ref,
    m_ref, pat_ref, ua, ub, mask, umask, strip, l1, l11, l2, invb,
    recv_sem, send_sem, strip_recv, strip_send, x_recv, x_send, inv_recv, inv_send, own_sem, in_sem,
):
    row, col = lax.axis_index("row"), lax.axis_index("col")
    rows, cols = m_ref.shape
    half = rows // 2
    part = rows // SPLIT
    slabs = cols // LANES
    per_tile = width // LANES
    steps = slabs // TREES * SPLIT

    def load(i):
        at = pl.ds(0, width) if i == 0 else pl.ds(width, cols - width)
        return pltpu.make_async_copy(m_hbm.at[:, at], m_ref.at[:, at], in_sem.at[i])

    pattern_load = pltpu.make_async_copy(pat_hbm, pat_ref, in_sem.at[2])
    pattern_load.start()
    load(0).start()
    load(1).start()

    barrier = pltpu.get_barrier_semaphore()
    dims = grid_of(n_row)
    expected = jnp.int32(n_col - 1)
    stride = n_row
    for size in dims:
        stride = stride // size
        place = (row // stride) % size
        for ok, other in ((place > 0, row - stride), (place < size - 1, row + stride)):
            expected = expected + ok.astype(jnp.int32)

            @pl.when(ok)
            def _(other=other):
                pl.semaphore_signal(barrier, inc=1, device_id={"row": other}, device_id_type=MESH)

    for c in range(n_col):
        @pl.when(col != c)
        def _(c=c):
            pl.semaphore_signal(barrier, inc=1, device_id={"col": jnp.int32(c)}, device_id_type=MESH)

    blocks = pat_ref.shape[1]

    def iota(shape, axis):
        return lax.broadcasted_iota(jnp.int32, shape, axis)

    def ones_where(condition):
        return jnp.where(condition, 1.0, 0.0).astype(BF16)

    def expand(tile):
        lane = iota((LANES, cols), 1)
        first = iota((LANES, cols), 0) * (cols // blocks)
        return jnp.dot(
            tile, ones_where((lane >= first) & (lane < first + cols // blocks)), preferred_element_type=F32
        )[0:2]

    pattern_load.wait()
    padded = jnp.dot(
        pat_ref[...].astype(F32).astype(BF16),
        ones_where(iota((blocks, LANES), 0) == iota((blocks, LANES), 1)),
        preferred_element_type=F32,
    ).astype(BF16)
    own = jnp.dot(
        ones_where(iota((STRIP, 2), 0) == iota((STRIP, 2), 1)), padded, preferred_element_type=F32
    ).astype(BF16)
    mask[...] = expand(own)

    @pl.when(row == 1)
    def _():
        strip[...] = own

    for skip, buffer in ((0, ua), (1, ub)):
        @pl.when((col == skip) & (row != skip))
        def _(buffer=buffer):
            buffer[0:per_tile] = jnp.zeros((per_tile, SPLIT, part, LANES), BF16)

    def source(dst, k):
        tile, sub = k // SPLIT, k % SPLIT
        at = pl.ds(pl.multiple_of(tile * width, width), width)
        keep = mask[:, at]
        keep = jnp.where(sub >= SPLIT // 2, keep[1:2], keep[0:1])
        values = m_ref[pl.ds(pl.multiple_of(sub * part, part), part), at].astype(F32)
        values = (values * keep).astype(BF16)
        for i in range(per_tile):
            dst[per_tile * tile + i, sub, :, :] = values[:, i * LANES:(i + 1) * LANES]

    load(0).wait()
    pl.semaphore_wait(barrier, expected)

    shard = inv_ref.shape[1]
    for k in range(2):
        mine = invb.at[pl.ds(pl.multiple_of(col * shard, 16), shard)]

        @pl.when(col != k)
        def _(k=k, mine=mine):
            pltpu.make_async_remote_copy(
                inv_ref.at[k], mine, inv_send.at[k], inv_recv.at[col],
                device_id={"col": jnp.int32(k)}, device_id_type=MESH,
            ).start()

        @pl.when(col == k)
        def _(k=k, mine=mine):
            pltpu.make_async_copy(inv_ref.at[k], mine, own_sem).start()

    def wait_inverse():
        pltpu.make_async_copy(
            inv_ref.at[0], invb.at[pl.ds(pl.multiple_of(col * shard, 16), shard)], own_sem
        ).wait()
        for c in range(n_col):
            @pl.when(col != c)
            def _(c=c):
                pltpu.make_async_remote_copy(
                    inv_ref.at[0], invb.at[pl.ds(c * shard, shard)], inv_send.at[0], inv_recv.at[c],
                    device_id={"col": jnp.int32(c)}, device_id_type=MESH,
                ).wait_recv()

    def to_columns(buffer, which, root, act):
        for c in range(n_col):
            if c != root:
                act(pltpu.make_async_remote_copy(
                    buffer, buffer, x_send.at[which, c], x_recv.at[which],
                    device_id={"col": jnp.int32(c)}, device_id_type=MESH,
                ))

    def from_column(buffer, which, root):
        @pl.when(col != root)
        def _():
            pltpu.make_async_remote_copy(
                buffer, buffer, x_send.at[which, root], x_recv.at[which],
                device_id={"col": jnp.int32(root)}, device_id_type=MESH,
            ).wait_recv()

    def tile_of(ref, j):
        parts = [
            jnp.concatenate([ref[per_tile * j + i, p, :, :] for i in range(per_tile)], axis=1)
            for p in range(SPLIT)
        ]
        return jnp.concatenate(parts, axis=0)

    def two(top, bottom):
        return jnp.concatenate(
            [jnp.broadcast_to(top, (half, width)), jnp.broadcast_to(bottom, (half, width))], axis=0
        )

    def columns(j):
        return pl.ds(pl.multiple_of(j * width, width), width)

    def mask_of(j, ref=mask):
        keep = ref[:, columns(j)]
        return two(keep[0:1], keep[1:2])

    def upper_mask(j):
        return mask_of(j, umask)

    def dot(a, b):
        return jnp.dot(a, b, preferred_element_type=F32)

    def dot_t(a, b):
        return lax.dot_general(a, b, (((1,), (1,)), ((), ())), preferred_element_type=F32)

    def make_l1():
        @pl.when(col < 2)
        def _():
            wait_inverse()

        @pl.when(col == 0)
        def _():
            keep = mask_of(0)
            tile = (m_ref[:, 0:width].astype(F32) * keep).astype(BF16)
            alive = (row > 0).astype(F32)
            l1[...] = (dot_t(tile, invb[...]) * (keep * alive)).astype(BF16)
            to_columns(l1, 0, 0, lambda copy: copy.start())

    def make_l2():
        umask[...] = expand(strip[...])

        @pl.when(col == 0)
        def _():
            l11[...] = (dot_t(tile_of(ub, 0), invb[...]) * upper_mask(0)).astype(BF16)
            to_columns(l11, 1, 0, lambda copy: copy.start())

        from_column(l1, 0, 0)

        @pl.when(col == 1)
        def _():
            keep = mask_of(0)
            one = ((m_ref[:, 0:width].astype(F32) - dot(l1[...], tile_of(ua, 0))) * keep).astype(BF16)
            alive = (row > 1).astype(F32)
            l2[...] = (dot_t(one, invb[...]) * (keep * alive)).astype(BF16)
            to_columns(l2, 2, 1, lambda copy: copy.start())

    def update(j):
        upper = tile_of(ua, j)
        row_one = ((tile_of(ub, j).astype(F32) - dot(l11[...], upper)) * upper_mask(j)).astype(BF16)
        total = m_ref[:, columns(j)].astype(F32) - dot(l1[...], upper) - dot(l2[...], row_one)
        out_ref[:, columns(j)] = (total * mask_of(j)).astype(BF16)

    plans, deepest = [], 0
    for t, parents in enumerate(all_trees(n_row)):
        packed, depth = pack_tree(parents)
        deepest = max(deepest, LAG * depth)
        code = select(packed, row)
        depth, code = code % 32, code // 32
        count, code = code % 4, code // 4
        plans.append((t, depth, count, (code % 64, (code // 64) % 64, code // 4096)))

    def chunk(t, k):
        buffer = ua if t < TREES else ub
        return buffer.at[TREES * (k // SPLIT) + t % TREES, k % SPLIT]

    def tree_copy(t, k, j, target):
        return pltpu.make_async_remote_copy(
            chunk(t, k), chunk(t, k), send_sem.at[t, j], recv_sem.at[t, k],
            device_id={"row": target}, device_id_type=MESH,
        )

    def strip_copy(j, target):
        return pltpu.make_async_remote_copy(
            strip, strip, strip_send.at[j], strip_recv, device_id={"row": target}, device_id_type=MESH,
        )

    def skipped(t):
        return col == t // TREES

    @pl.loop(0, steps + deepest + 1)
    def _(now):
        for r, buffer in ((0, ua), (1, ub)):
            @pl.when((row == r) & (now < steps))
            def _(buffer=buffer):
                source(buffer, now)

        for i in range(2 * TREES):
            t, depth, count, children = plans[(i % 2) * TREES + i // 2]
            k = now - LAG * depth

            if t == TREES:
                @pl.when(k == 0)
                def _(depth=depth, count=count, children=children):
                    @pl.when(depth > 0)
                    def _():
                        strip_copy(0, children[0]).wait_recv()

                    for j in range(3):
                        @pl.when(count > j)
                        def _(j=j):
                            strip_copy(j, children[j]).start()

            @pl.when((k >= jnp.where(skipped(t), SPLIT, 0)) & (k < steps))
            def _(t=t, depth=depth, count=count, children=children, k=k):
                @pl.when(depth > 0)
                def _():
                    tree_copy(t, k, 0, children[0]).wait_recv()

                for j in range(3):
                    @pl.when(count > j)
                    def _(j=j):
                        tree_copy(t, k, j, children[j]).start()

        @pl.when(now == 1)
        def _():
            load(1).wait()
            make_l1()

        done = now - (SPLIT + deepest)

        @pl.when(done == -1)
        def _():
            make_l2()

        @pl.when(done == 0)
        def _():
            from_column(l11, 1, 0)
            from_column(l2, 2, 1)

        @pl.when((done >= 0) & (done % SPLIT == 0))
        def _():
            update(done // SPLIT)

    @pl.when((col == 0) & (row >= 1))
    def _():
        out_ref[:, 0:width] = l1[...]

    @pl.when((col == 1) & (row >= 2))
    def _():
        out_ref[:, 0:width] = l2[...]

    for t, depth, count, children in plans:
        buffer = ua if t < TREES else ub
        each = slabs // TREES
        for j in range(3):
            def left(n, t=t, j=j, buffer=buffer, children=children):
                pltpu.make_async_remote_copy(
                    buffer.at[0:n], buffer.at[0:n], send_sem.at[t, j], recv_sem.at[t, 0],
                    device_id={"row": children[j]}, device_id_type=MESH,
                ).wait_send()

            @pl.when((count > j) & skipped(t))
            def _(left=left):
                left(each - 1)

            @pl.when((count > j) & jnp.logical_not(skipped(t)))
            def _(left=left):
                left(each)

            if t == TREES:
                @pl.when(count > j)
                def _(j=j, children=children):
                    strip_copy(j, children[j]).wait_send()

    for k in range(2):
        @pl.when(col != k)
        def _(k=k):
            pltpu.make_async_remote_copy(
                inv_ref.at[k], invb.at[0:shard], inv_send.at[k], inv_recv.at[0],
                device_id={"col": jnp.int32(k)}, device_id_type=MESH,
            ).wait_send()

    @pl.when(col == 0)
    def _():
        to_columns(l1, 0, 0, lambda copy: copy.wait_send())
        to_columns(l11, 1, 0, lambda copy: copy.wait_send())

    @pl.when(col == 1)
    def _():
        to_columns(l2, 2, 1, lambda copy: copy.wait_send())


def solution(mesh):
    n_row, n_col = mesh.shape["row"], mesh.shape["col"]

    def shards(matrix, pattern, inverse):
        rows, cols = matrix.shape
        width = inverse.shape[1]
        slabs = cols // LANES
        steps = slabs // TREES * SPLIT
        turned = jnp.swapaxes(inverse, 1, 2)
        flops = 2 * rows * cols * width * 3
        return pl.pallas_call(
            functools.partial(kernel, n_row, n_col, width),
            out_shape=jax.ShapeDtypeStruct(matrix.shape, BF16),
            in_specs=[pl.BlockSpec(memory_space=pltpu.HBM)] * 3,
            out_specs=pl.BlockSpec(memory_space=pltpu.VMEM),
            scratch_shapes=[
                pltpu.VMEM((rows, cols), BF16),
                pltpu.VMEM(pattern.shape, jnp.int32),
                pltpu.VMEM((slabs, SPLIT, rows // SPLIT, LANES), BF16),
                pltpu.VMEM((slabs, SPLIT, rows // SPLIT, LANES), BF16),
                pltpu.VMEM((2, cols), F32),
                pltpu.VMEM((2, cols), F32),
                pltpu.VMEM((STRIP, LANES), BF16),
                pltpu.VMEM((rows, width), BF16),
                pltpu.VMEM((width, width), BF16),
                pltpu.VMEM((rows, width), BF16),
                pltpu.VMEM((width, width), BF16),
                pltpu.SemaphoreType.DMA((2 * TREES, steps)),
                pltpu.SemaphoreType.DMA((2 * TREES, 3)),
                pltpu.SemaphoreType.DMA,
                pltpu.SemaphoreType.DMA((3,)),
                pltpu.SemaphoreType.DMA((3,)),
                pltpu.SemaphoreType.DMA((3, n_col)),
                pltpu.SemaphoreType.DMA((n_col,)),
                pltpu.SemaphoreType.DMA((2,)),
                pltpu.SemaphoreType.DMA,
                pltpu.SemaphoreType.DMA((3,)),
            ],
            compiler_params=pltpu.CompilerParams(
                collective_id=0, has_side_effects=True, vmem_limit_bytes=62 * 1024 * 1024
            ),
            cost_estimate=pl.CostEstimate(flops=flops, bytes_accessed=4 * rows * cols, transcendentals=0),
        )(matrix, pattern, turned)

    return jax.shard_map(
        shards,
        mesh=mesh,
        in_specs=(P("row", "col"), P("row", "col"), P(None, None, "col")),
        out_specs=P("row", "col"),
        check_vma=False,
    )
```
